512 devices in a mesh: tm: 8 (over x, y_hi), space: 64 (over z, y_lo, core).
Axes of the slice: x: 4, y: 8 (y_hi: 2, y_lo: 4; y = y_hi * 4 + y_lo), z: 8, core: 2. Of those that a mesh axis runs over, the one named last changes fastest.
Arguments:
- adjoint: float32 [8, 5, 256, 1024], P('tm', None, 'space'), may hold values from -6 to 6
- jac_x: float32 [8, 4, 5, 5, 256, 1024], P('tm', None, None, None, 'space'), may hold values from -4 to 4
- jac_local: float32 [8, 3, 5, 5, 256, 1024], P('tm', None, None, None, 'space'), may hold values from -4 to 4
- objective_gradient: float32 [8, 5, 256, 1024], P('tm', None, 'space'), may hold values from -6 to 6
- volume: float32 [256, 1024], P('space'), may hold values from 0.5 to 2
- face_lower: int32 [64, 1024], P('space'), may hold values from 0 to 1023, as said below
- face_upper: int32 [64, 1024], P('space'), may hold values from 0 to 1023, as said below
Outputs:
- adjoint_residual: float32 [8, 5, 256, 1024], P('tm', None, 'space')
The draws below stay inside these ranges and needn't reach their ends.
Inputs may be any that keep to these rules, and one draw needn't show every extreme that they name: `face_lower`: each row is a permutation of 0 to 1023; row 0 is never read. `face_upper`: each row is a permutation of 0 to 1023, and row s is the inverse permutation of face_lower row s+1 (the last row that of row 0, and never read).
All inputs are finite; a program needn't handle non-finite values.
Results may differ from the reference program's by a relative error of at most 0.000065.
Values sent between devices are 32-bit elements; how exact they have to be, the bound alone decides.
No kernel may reach another device: no remote copies, remote signals or barrier semaphores. Data moves between devices by JAX's collectives and lax.ppermute only.
A program may use at most 64 MiB of HBM per device.

```python
import math
import jax
import jax.numpy as jnp
from jax import lax

NT = 8
NF = 5
CX = 4
NY = 1024
NX = 256
N_SPACE = 64


def face_tables(key):
    keys = jax.random.split(key, N_SPACE)
    lower = jax.vmap(lambda single: jax.random.permutation(single, NY))(keys).astype(jnp.int32)
    inverse = jnp.argsort(lower, axis=1).astype(jnp.int32)
    upper = jnp.roll(inverse, -1, axis=0)
    return (lower, upper)


def draw_face_lower(key, part):
    return face_tables(key)[0]


def draw_face_upper(key, part):
    return face_tables(key)[1]


def block_scale(rng, extent, cuts, smallest, top_value):
    gain, own = 1.0, jax.random.fold_in(rng, 6)
    for axis_at, blocks in cuts:
        heights = jnp.exp(jax.random.uniform(jax.random.fold_in(own, axis_at), (blocks,), jnp.float32, smallest / len(cuts), top_value / len(cuts)))
        gain = gain * jnp.repeat(heights, extent[axis_at] // blocks).reshape([-1 if axis == axis_at else 1 for axis in range(len(extent))])
    return gain


def gaussian(key, extent, spread, reach, cuts=(), held_as=jnp.bfloat16):
    loudness = block_scale(key, extent, cuts, -0.22, 0.18) if cuts else 1.0
    drawn = jax.random.normal(key, extent, jnp.float32) * spread * loudness
    return jnp.minimum(jnp.maximum(drawn, -reach), reach).astype(held_as)


def setup_inputs(seed: int = 0) -> dict:
    streams_of = jax.random.split(jax.random.key(seed), 8)
    adjoint = gaussian(streams_of[0], (NT, NF, NX, NY), 1.0, 6.0, ((0, 8), (2, 64)), jnp.float32)
    jac_x = gaussian(streams_of[1], (NT, 4, NF, NF, NX, NY), 0.3, 4.0, ((0, 8), (4, 64)), jnp.float32)
    jac_local = gaussian(streams_of[2], (NT, 3, NF, NF, NX, NY), 0.3, 4.0, ((0, 8), (4, 64)), jnp.float32)
    objective_gradient = gaussian(streams_of[3], (NT, NF, NX, NY), 1.0, 6.0, ((0, 8), (2, 64)), jnp.float32)
    volume = jnp.clip(jnp.exp(math.log(2.0) - 1.3862944 * jax.random.uniform(streams_of[4], (NX, NY), jnp.float32) ** block_scale(streams_of[4], (NX, NY), ((0, 64),), -0.2, 0.2)), 0.5, 2.0)
    face_lower = draw_face_lower(jax.random.fold_in(streams_of[7], 71), 0)
    face_upper = draw_face_upper(jax.random.fold_in(streams_of[7], 71), 0)
    return dict(adjoint=adjoint, jac_x=jac_x, jac_local=jac_local, objective_gradient=objective_gradient, volume=volume, face_lower=face_lower, face_upper=face_upper)


def spectral_table():
    index = jnp.arange(NT)
    offset = index[:, None] - index[None, :]
    parity = jnp.where(offset % 2 == 0, 1.0, -1.0).astype(jnp.float32)
    mask = jnp.logical_and(offset != 0, jnp.abs(offset) * 2 != NT)
    safe = jnp.where(mask, offset, 1).astype(jnp.float32)
    first = jnp.where(mask, 0.5 * parity / jnp.tan(jnp.pi * safe / NT), 0.0)
    apart = offset != 0
    wide = jnp.where(apart, offset, 1).astype(jnp.float32)
    sine = jnp.sin(jnp.pi * wide / NT)
    second = jnp.where(apart, -0.5 * parity / (sine * sine), -(NT * NT + 2) / 12.0)
    return (first + 0.25 * second).astype(jnp.float32)


def extend(field, face_lower, face_upper):
    chans = field.shape[0]
    slabs = field.reshape(chans, N_SPACE, CX, NY)
    zeros = jnp.zeros((chans, 1, 2, NY), field.dtype)
    below = jnp.concatenate([zeros, slabs[:, :-1, CX - 2:]], axis=1)
    above = jnp.concatenate([slabs[:, 1:, :2], zeros], axis=1)
    lower_index = jnp.broadcast_to(face_lower[None, :, None, :], below.shape)
    upper_index = jnp.broadcast_to(face_upper[None, :, None, :], above.shape)
    below = jnp.take_along_axis(below, lower_index, axis=3)
    above = jnp.take_along_axis(above, upper_index, axis=3)
    return jnp.concatenate([below, slabs, above], axis=2)


def instance(args, face_lower, face_upper):
    psi, jac_x, jac_local = args
    ext_psi = extend(psi, face_lower, face_upper)
    ext_jac = extend(jac_x.reshape(100, NX, NY), face_lower, face_upper).reshape(4, NF, NF, N_SPACE, CX + 4, NY)
    q_terms = jnp.sum(ext_jac * ext_psi[None, :, None], axis=1)
    xpart = None
    for k_index, offset in enumerate((1, -1, 2, -2)):
        piece = q_terms[k_index, :, :, 2 - offset:2 - offset + CX, :]
        xpart = piece if xpart is None else xpart + piece
    xpart = xpart.reshape(NF, NX, NY)
    center = jnp.sum(jac_local[0] * psi[:, None], axis=0)
    plus_term = jnp.sum(jac_local[1] * psi[:, None], axis=0)
    minus_term = jnp.sum(jac_local[2] * psi[:, None], axis=0)
    zero_col = jnp.zeros((NF, NX, 1), psi.dtype)
    from_below = jnp.concatenate([zero_col, plus_term[:, :, :-1]], axis=2)
    from_above = jnp.concatenate([minus_term[:, :, 1:], zero_col], axis=2)
    local = center + from_below + from_above
    return local, xpart


def reference(adjoint, jac_x, jac_local, objective_gradient, volume, face_lower, face_upper):
    local, xpart = lax.map(lambda a: instance(a, face_lower, face_upper), (adjoint, jac_x, jac_local))
    table = spectral_table().astype(adjoint.dtype)
    spectral = jnp.einsum("st,sfxy->tfxy", table, adjoint, precision=lax.Precision.HIGHEST)
    return objective_gradient + local + xpart + 1.5 * volume[None, None] * spectral
```

```python
import jax
import jax.numpy as jnp
import numpy as np
from jax import lax
from jax.experimental import pallas as pl
from jax.experimental.pallas import tpu as pltpu
from jax.sharding import PartitionSpec as P

NT = 8
NF = 5
PAIRS = NT // 2
VMEM = pl.BlockSpec(memory_space=pltpu.VMEM)
SMEM = pl.BlockSpec(memory_space=pltpu.SMEM)
ANY = pl.BlockSpec(memory_space=pl.ANY)


def spectral_table(count):
    index = np.arange(count)
    offset = index[:, None] - index[None, :]
    parity = np.where(offset % 2 == 0, 1.0, -1.0)
    mask = np.logical_and(offset != 0, np.abs(offset) * 2 != count)
    safe = np.where(mask, offset, 1)
    first = np.where(mask, 0.5 * parity / np.tan(np.pi * safe / count), 0.0)
    apart = offset != 0
    wide = np.where(apart, offset, 1)
    sine = np.sin(np.pi * wide / count)
    second = np.where(apart, -0.5 * parity / (sine * sine), -(count * count + 2) / 12.0)
    return (first + 0.25 * second).astype(np.float32)


def stencil_kernel(space_ref, adj_ref, jx_hbm, jl_hbm, obj_ref, part_ref, near_ref, far_ref,
                   jx, jl, ext, side, sems):
    copies = [pltpu.make_async_copy(jx_hbm.at[k], jx.at[k], sems.at[k]) for k in range(4)]
    copies += [pltpu.make_async_copy(jl_hbm.at[k], jl.at[k], sems.at[4 + k]) for k in range(3)]
    for copy in copies:
        copy.start()
    cells = adj_ref.shape[2]
    ext[...] = jnp.zeros_like(ext)
    side[...] = jnp.zeros_like(side)
    for k, offset in enumerate((1, -1, 2, -2)):
        copies[k].wait()
        for b in range(NF):
            q = jx[k, 0, b] * adj_ref[0]
            for a in range(1, NF):
                q = q + jx[k, a, b] * adj_ref[a]
            ext[b, 2 + offset:6 + offset, :] += q
    even = space_ref[0] % 2 == 0
    for b in range(NF):
        below = ext[b, 0:2, :]
        above = ext[b, 6:8, :]
        near_ref[b] = jnp.where(even, above, below)
        far_ref[b] = jnp.where(even, below, above)
    lane = lax.broadcasted_iota(jnp.int32, (8, cells), 1)
    for k in range(3):
        copies[4 + k].wait()
        for b in range(NF):
            q = jl[k, 0, b] * adj_ref[0]
            for a in range(1, NF):
                q = q + jl[k, a, b] * adj_ref[a]
            if k == 0:
                ext[b, 2:6, :] += q
            else:
                side[b, 2:6, :] = q
                moved = pltpu.roll(side[b], 1 if k == 1 else cells - 1, 1)
                ext[b] += jnp.where(lane == (0 if k == 1 else cells - 1), 0.0, moved)
    for b in range(NF):
        part_ref[b] = obj_ref[b] + ext[b, 2:6, :]


def combine_kernel(coef_ref, own_ref, other_ref, out_ref):
    for j in range(PAIRS):
        out_ref[j] = coef_ref[0, j] * own_ref[...] + coef_ref[1, j] * other_ref[...]


def finish_kernel(space_ref, part_ref, spec_ref, vol_ref, near_ref, far_ref, low_ref, up_ref, out_ref, halo, moved):
    odd = space_ref[0] % 2 == 1
    cells = vol_ref.shape[1]
    halo[...] = jnp.zeros_like(halo)
    for b in range(NF):
        row = 4 * (b % 2)
        halo[b // 2, row:row + 2, :] = jnp.where(odd, near_ref[b], far_ref[b])
        halo[b // 2, row + 2:row + 4, :] = jnp.where(odd, far_ref[b], near_ref[b])
    groups = halo.shape[0]
    chunks = cells // 128
    from_low = lax.broadcasted_iota(jnp.int32, (8, 128), 0) % 4 < 2
    for j in range(chunks):
        here = slice(128 * j, 128 * (j + 1))
        low = jnp.broadcast_to(low_ref[0:1, here], (8, 128))
        up = jnp.broadcast_to(up_ref[0:1, here], (8, 128))
        index = jnp.where(from_low, low, up)
        lane = index % 128
        chunk = index // 128
        for g in range(groups):
            total = None
            for c in range(chunks):
                piece = jnp.take_along_axis(halo[g, :, 128 * c:128 * (c + 1)], lane, axis=1, mode="promise_in_bounds")
                total = piece if c == 0 else jnp.where(chunk == c, piece, total)
            moved[g, :, here] = total
    scale = 1.5 * vol_ref[...]
    for b in range(NF):
        row = 4 * (b % 2)
        spectral = spec_ref[0, b]
        for j in range(1, PAIRS):
            spectral = spectral + spec_ref[j, b]
        out_ref[b] = part_ref[b] + moved[b // 2, row:row + 4, :] + scale * spectral


def body(adjoint, jac_x, jac_local, objective_gradient, volume, face_lower, face_upper):
    _, _, layers, cells = adjoint.shape
    space = lax.axis_index("space")
    here = lax.axis_index("tm")
    count = lax.axis_size("space")
    field = jax.ShapeDtypeStruct((NF, layers, cells), jnp.float32)
    face = jax.ShapeDtypeStruct((NF, 2, cells), jnp.float32)
    own = adjoint[0]
    other = lax.ppermute(own, "tm", [(i, i ^ 1) for i in range(NT)])
    space_at = space.reshape(1).astype(jnp.int32)
    part, near, far = pl.pallas_call(
        stencil_kernel,
        out_shape=(field, face, face),
        in_specs=[SMEM, VMEM, ANY, ANY, VMEM],
        out_specs=(VMEM, VMEM, VMEM),
        scratch_shapes=[
            pltpu.VMEM((4, NF, NF, layers, cells), jnp.float32),
            pltpu.VMEM((3, NF, NF, layers, cells), jnp.float32),
            pltpu.VMEM((NF, 8, cells), jnp.float32),
            pltpu.VMEM((NF, 8, cells), jnp.float32),
            pltpu.SemaphoreType.DMA((7,)),
        ],
        cost_estimate=pl.CostEstimate(flops=350 * layers * cells, bytes_accessed=3_000_000, transcendentals=0),
        compiler_params=pltpu.CompilerParams(vmem_limit_bytes=16 * 2**20),
        name="stencil",
    )(space_at, own, jac_x[0], jac_local[0], objective_gradient[0])
    near = lax.ppermute(near, "space", [(i, i ^ 1) for i in range(count)])
    far = lax.ppermute(far, "space", [pair for i in range(1, count - 1, 2) for pair in ((i, i + 1), (i + 1, i))])
    table = spectral_table(NT)
    mine = np.stack([table[i, i % 2::2] for i in range(NT)])
    theirs = np.stack([table[i ^ 1, i % 2::2] for i in range(NT)])
    coefficients = lax.dynamic_index_in_dim(jnp.asarray(np.stack([mine, theirs], 1)), here, 0, keepdims=False)
    combined = pl.pallas_call(
        combine_kernel,
        out_shape=jax.ShapeDtypeStruct((PAIRS, NF, layers, cells), jnp.float32),
        in_specs=[SMEM, VMEM, VMEM],
        out_specs=VMEM,
        cost_estimate=pl.CostEstimate(flops=12 * NF * layers * cells, bytes_accessed=500_000, transcendentals=0),
        name="combine",
    )(coefficients, own, other)
    groups = [list(range(parity, NT, 2)) for parity in range(2)]
    spectral = lax.all_to_all(combined, "tm", 0, 0, tiled=True, axis_index_groups=groups)
    out = pl.pallas_call(
        finish_kernel,
        out_shape=field,
        in_specs=[SMEM, VMEM, VMEM, VMEM, VMEM, VMEM, VMEM, VMEM],
        out_specs=VMEM,
        scratch_shapes=[
            pltpu.VMEM(((NF + 1) // 2, 8, cells), jnp.float32),
            pltpu.VMEM(((NF + 1) // 2, 8, cells), jnp.float32),
        ],
        cost_estimate=pl.CostEstimate(flops=30 * NF * layers * cells, bytes_accessed=800_000, transcendentals=0),
        name="finish",
    )(space_at, part, spectral, volume, near, far, face_lower, face_upper)
    return out[None]


def solution(mesh):
    in_specs = (
        P("tm", None, "space", None),
        P("tm", None, None, None, "space", None),
        P("tm", None, None, None, "space", None),
        P("tm", None, "space", None),
        P("space", None),
        P("space", None),
        P("space", None),
    )
    out_specs = P("tm", None, "space", None)
    return jax.shard_map(body, mesh=mesh, in_specs=in_specs, out_specs=out_specs, check_vma=False)
```

```python
import jax
import jax.numpy as jnp
import numpy as np
from jax import lax
from jax.experimental import pallas as pl
from jax.experimental.pallas import tpu as pltpu
from jax.sharding import PartitionSpec as P

NT = 8
NF = 5
PAIRS = NT // 2
VMEM = pl.BlockSpec(memory_space=pltpu.VMEM)
HBM = pl.BlockSpec(memory_space=pltpu.HBM)


def spectral_table(count):
    index = np.arange(count)
    offset = index[:, None] - index[None, :]
    parity = np.where(offset % 2 == 0, 1.0, -1.0)
    mask = np.logical_and(offset != 0, np.abs(offset) * 2 != count)
    safe = np.where(mask, offset, 1)
    first = np.where(mask, 0.5 * parity / np.tan(np.pi * safe / count), 0.0)
    apart = offset != 0
    wide = np.where(apart, offset, 1)
    sine = np.sin(np.pi * wide / count)
    second = np.where(apart, -0.5 * parity / (sine * sine), -(count * count + 2) / 12.0)
    return (first + 0.25 * second).astype(np.float32)


def products(fields, blocks, k, b, here):
    total = blocks[k, 0, b, :, here] * fields[0]
    for a in range(1, NF):
        total = total + blocks[k, a, b, :, here] * fields[a]
    return total


def across_kernel(adj_hbm, jac_hbm, own_ref, inner_ref, near_ref, far_ref, jac, ext, sems):
    first = pltpu.make_async_copy(adj_hbm, own_ref, sems.at[0])
    first.start()
    copies = [pltpu.make_async_copy(jac_hbm.at[k], jac.at[k], sems.at[1 + k]) for k in range(4)]
    for copy in copies:
        copy.start()
    cells = own_ref.shape[2]
    ext[...] = jnp.zeros_like(ext)
    first.wait()
    for k, offset in enumerate((1, -1, 2, -2)):
        copies[k].wait()
        for at in range(0, cells, 128):
            here = slice(at, at + 128)
            fields = [own_ref[a, :, here] for a in range(NF)]
            for b in range(NF):
                ext[b, 2 + offset:6 + offset, here] += products(fields, jac, k, b, here)
    even = lax.axis_index("space") % 2 == 0
    for b in range(NF):
        below = ext[b, 0:2, :]
        above = ext[b, 6:8, :]
        inner_ref[b] = ext[b, 2:6, :]
        near_ref[b] = jnp.where(even, above, below)
        far_ref[b] = jnp.where(even, below, above)


def along_kernel(own_ref, inner_ref, jac_hbm, obj_hbm, part_ref, jac, obj, side, sems):
    copies = [pltpu.make_async_copy(jac_hbm.at[k], jac.at[k], sems.at[k]) for k in range(3)]
    last = pltpu.make_async_copy(obj_hbm, obj, sems.at[3])
    for copy in copies[1:]:
        copy.start()
    copies[0].start()
    last.start()
    cells = own_ref.shape[2]
    side[...] = jnp.zeros_like(side)
    lane = lax.broadcasted_iota(jnp.int32, (8, cells), 1)
    for k in (1, 2, 0):
        copies[k].wait()
        for at in range(0, cells, 128):
            here = slice(at, at + 128)
            fields = [own_ref[a, :, here] for a in range(NF)]
            for b in range(NF):
                total = products(fields, jac, k, b, here)
                if k == 0:
                    part_ref[b, :, here] = total
                else:
                    side[k - 1, b, 0:4, here] = total
    last.wait()
    for b in range(NF):
        plus = jnp.where(lane == 0, 0.0, pltpu.roll(side[0, b], 1, 1))
        minus = jnp.where(lane == cells - 1, 0.0, pltpu.roll(side[1, b], cells - 1, 1))
        side[0, b] = plus + minus
        part_ref[b] = part_ref[b] + obj[b] + inner_ref[b] + side[0, b, 0:4, :]


def combine_kernel(own_ref, other_ref, out_ref):
    at = lax.axis_index("tm")
    odd = at % 2 == 1
    table = spectral_table(NT)
    for j in range(PAIRS):
        ours = float(table[0, 2 * j])
        theirs = jnp.where(odd, float(table[0, (2 * j + 1) % NT]), float(table[1, 2 * j]))
        out_ref[(at // 2 + j) % PAIRS] = ours * own_ref[...] + theirs * other_ref[...]


def faces_kernel(part_ref, near_ref, far_ref, low_ref, up_ref, out_ref, halo, moved):
    odd = lax.axis_index("space") % 2 == 1
    cells = low_ref.shape[1]
    halo[...] = jnp.zeros_like(halo)
    for b in range(NF):
        row = 4 * (b % 2)
        halo[b // 2, row:row + 2, :] = jnp.where(odd, near_ref[b], far_ref[b])
        halo[b // 2, row + 2:row + 4, :] = jnp.where(odd, far_ref[b], near_ref[b])
    groups = halo.shape[0]
    chunks = cells // 128
    from_low = lax.broadcasted_iota(jnp.int32, (8, 128), 0) % 4 < 2
    for j in range(chunks):
        here = slice(128 * j, 128 * (j + 1))
        low = jnp.broadcast_to(low_ref[0:1, here], (8, 128))
        up = jnp.broadcast_to(up_ref[0:1, here], (8, 128))
        index = jnp.where(from_low, low, up)
        lane = index % 128
        chunk = index // 128
        for g in range(groups):
            total = None
            for c in range(chunks):
                piece = jnp.take_along_axis(halo[g, :, 128 * c:128 * (c + 1)], lane, axis=1, mode="promise_in_bounds")
                total = piece if c == 0 else jnp.where(chunk == c, piece, total)
            moved[g, :, here] = total
    for b in range(NF):
        row = 4 * (b % 2)
        out_ref[b] = part_ref[b] + moved[b // 2, row:row + 4, :]


def finish_kernel(part_ref, spec_ref, vol_ref, out_ref):
    scale = 1.5 * vol_ref[...]
    for b in range(NF):
        spectral = spec_ref[0, b]
        for j in range(1, PAIRS):
            spectral = spectral + spec_ref[j, b]
        out_ref[b] = part_ref[b] + scale * spectral


def kernel_call(kernel, name, out_shape, in_specs, scratch=(), out_specs=None, limit=2**20, flops=0, moved=0):
    if out_specs is None:
        out_specs = jax.tree.map(lambda _: VMEM, out_shape)
    return pl.pallas_call(
        kernel,
        out_shape=out_shape,
        in_specs=in_specs,
        out_specs=out_specs,
        scratch_shapes=scratch,
        cost_estimate=pl.CostEstimate(flops=flops, bytes_accessed=moved, transcendentals=0),
        compiler_params=pltpu.CompilerParams(vmem_limit_bytes=limit),
        name=name,
    )


def body(adjoint, jac_x, jac_local, objective_gradient, volume, face_lower, face_upper):
    _, _, layers, cells = adjoint.shape
    count = lax.axis_size("space")
    block = NF * layers * cells
    field = jax.ShapeDtypeStruct((NF, layers, cells), jnp.float32)
    face = jax.ShapeDtypeStruct((NF, 2, cells), jnp.float32)
    other = lax.ppermute(adjoint[0], "tm", [(i, i ^ 1) for i in range(NT)])
    own, inner, near, far = kernel_call(
        across_kernel, "across", (field, field, face, face), [HBM, HBM],
        [
            pltpu.VMEM((4, NF, NF, layers, cells), jnp.float32),
            pltpu.VMEM((NF, 8, cells), jnp.float32),
            pltpu.SemaphoreType.DMA((5,)),
        ],
        limit=3 * 2**20, flops=40 * block, moved=84 * block,
    )(adjoint[0], jac_x[0])
    far = lax.ppermute(far, "space", [pair for i in range(1, count - 1, 2) for pair in ((i, i + 1), (i + 1, i))])
    combined = kernel_call(
        combine_kernel, "combine", jax.ShapeDtypeStruct((PAIRS, NF, layers, cells), jnp.float32), [VMEM, VMEM],
        flops=12 * block, moved=24 * block,
    )(own, other)
    groups = [list(range(parity, NT, 2)) for parity in range(2)]
    spectral = lax.all_to_all(combined, "tm", 0, 0, tiled=True, axis_index_groups=groups)
    near = lax.ppermute(near, "space", [(i, i ^ 1) for i in range(count)])
    part = kernel_call(
        along_kernel, "along", field, [VMEM, VMEM, HBM, HBM],
        [
            pltpu.VMEM((3, NF, NF, layers, cells), jnp.float32),
            pltpu.VMEM((NF, layers, cells), jnp.float32),
            pltpu.VMEM((2, NF, 8, cells), jnp.float32),
            pltpu.SemaphoreType.DMA((4,)),
        ],
        limit=3 * 2**20, flops=30 * block, moved=80 * block,
    )(own, inner, jac_local[0], objective_gradient[0])
    part = kernel_call(
        faces_kernel, "faces", field, [VMEM] * 5,
        [
            pltpu.VMEM(((NF + 1) // 2, 8, cells), jnp.float32),
            pltpu.VMEM(((NF + 1) // 2, 8, cells), jnp.float32),
        ],
        flops=20 * block, moved=20 * block,
    )(part, near, far, face_lower, face_upper)
    out = kernel_call(
        finish_kernel, "finish", field, [VMEM] * 3, flops=5 * block, moved=24 * block,
    )(part, spectral, volume)
    return out[None]


def solution(mesh):
    in_specs = (
        P("tm", None, "space", None),
        P("tm", None, None, None, "space", None),
        P("tm", None, None, None, "space", None),
        P("tm", None, "space", None),
        P("space", None),
        P("space", None),
        P("space", None),
    )
    out_specs = P("tm", None, "space", None)
    return jax.shard_map(body, mesh=mesh, in_specs=in_specs, out_specs=out_specs, check_vma=False)
```

```python
import jax
import jax.numpy as jnp
import numpy as np
from jax import lax
from jax.experimental import pallas as pl
from jax.experimental.pallas import tpu as pltpu
from jax.sharding import PartitionSpec as P

NT = 8
NF = 5
PAIRS = NT // 2
VMEM = pl.BlockSpec(memory_space=pltpu.VMEM)
HBM = pl.BlockSpec(memory_space=pltpu.HBM)


def spectral_table(count):
    index = np.arange(count)
    offset = index[:, None] - index[None, :]
    parity = np.where(offset % 2 == 0, 1.0, -1.0)
    mask = np.logical_and(offset != 0, np.abs(offset) * 2 != count)
    safe = np.where(mask, offset, 1)
    first = np.where(mask, 0.5 * parity / np.tan(np.pi * safe / count), 0.0)
    apart = offset != 0
    wide = np.where(apart, offset, 1)
    sine = np.sin(np.pi * wide / count)
    second = np.where(apart, -0.5 * parity / (sine * sine), -(count * count + 2) / 12.0)
    return (first + 0.25 * second).astype(np.float32)


def products(fields, blocks, k, b, here):
    total = blocks[k, 0, b, :, here] * fields[0]
    for a in range(1, NF):
        total = total + blocks[k, a, b, :, here] * fields[a]
    return total


def across_kernel(adj_hbm, jac_hbm, own_ref, inner_ref, near_ref, far_ref, jac, ext, sems):
    first = pltpu.make_async_copy(adj_hbm, own_ref, sems.at[0])
    first.start()
    copies = [pltpu.make_async_copy(jac_hbm.at[k], jac.at[k], sems.at[1 + k]) for k in range(4)]
    for copy in copies:
        copy.start()
    cells = own_ref.shape[2]
    ext[...] = jnp.zeros_like(ext)
    first.wait()
    for k, offset in enumerate((1, -1, 2, -2)):
        copies[k].wait()
        for at in range(0, cells, 128):
            here = slice(at, at + 128)
            fields = [own_ref[a, :, here] for a in range(NF)]
            for b in range(NF):
                ext[b, 2 + offset:6 + offset, here] += products(fields, jac, k, b, here)
    even = lax.axis_index("space") % 2 == 0
    for b in range(NF):
        below = ext[b, 0:2, :]
        above = ext[b, 6:8, :]
        inner_ref[b] = ext[b, 2:6, :]
        near_ref[b] = jnp.where(even, above, below)
        far_ref[b] = jnp.where(even, below, above)


def along_kernel(own_ref, inner_ref, jac_ref, obj_ref, part_ref, side):
    cells = own_ref.shape[2]
    side[...] = jnp.zeros_like(side)
    for at in range(0, cells, 128):
        here = slice(at, at + 128)
        fields = [own_ref[a, :, here] for a in range(NF)]
        for b in range(NF):
            part_ref[b, :, here] = obj_ref[b, :, here] + inner_ref[b, :, here] + products(fields, jac_ref, 0, b, here)
            for k in (1, 2):
                side[k - 1, b, 0:4, here] = products(fields, jac_ref, k, b, here)
    lane = lax.broadcasted_iota(jnp.int32, (8, cells), 1)
    for b in range(NF):
        plus = jnp.where(lane == 0, 0.0, pltpu.roll(side[0, b], 1, 1))
        minus = jnp.where(lane == cells - 1, 0.0, pltpu.roll(side[1, b], cells - 1, 1))
        side[0, b] = plus + minus
        part_ref[b] = part_ref[b] + side[0, b, 0:4, :]


def combine_kernel(own_ref, other_ref, out_ref):
    at = lax.axis_index("tm")
    odd = at % 2 == 1
    table = spectral_table(NT)
    for j in range(PAIRS):
        ours = float(table[0, 2 * j])
        theirs = jnp.where(odd, float(table[0, (2 * j + 1) % NT]), float(table[1, 2 * j]))
        out_ref[(at // 2 + j) % PAIRS] = ours * own_ref[...] + theirs * other_ref[...]


def after_kernel(near_ref, far_ref, near_out_ref, far_out_ref):
    near_out_ref[...] = near_ref[...]
    far_out_ref[...] = far_ref[...]


def faces_kernel(part_ref, near_ref, far_ref, low_ref, up_ref, out_ref, halo, moved):
    odd = lax.axis_index("space") % 2 == 1
    cells = low_ref.shape[1]
    halo[...] = jnp.zeros_like(halo)
    for b in range(NF):
        row = 4 * (b % 2)
        halo[b // 2, row:row + 2, :] = jnp.where(odd, near_ref[b], far_ref[b])
        halo[b // 2, row + 2:row + 4, :] = jnp.where(odd, far_ref[b], near_ref[b])
    groups = halo.shape[0]
    chunks = cells // 128
    from_low = lax.broadcasted_iota(jnp.int32, (8, 128), 0) % 4 < 2
    for j in range(chunks):
        here = slice(128 * j, 128 * (j + 1))
        low = jnp.broadcast_to(low_ref[0:1, here], (8, 128))
        up = jnp.broadcast_to(up_ref[0:1, here], (8, 128))
        index = jnp.where(from_low, low, up)
        lane = index % 128
        chunk = index // 128
        for g in range(groups):
            total = None
            for c in range(chunks):
                piece = jnp.take_along_axis(halo[g, :, 128 * c:128 * (c + 1)], lane, axis=1, mode="promise_in_bounds")
                total = piece if c == 0 else jnp.where(chunk == c, piece, total)
            moved[g, :, here] = total
    for b in range(NF):
        row = 4 * (b % 2)
        out_ref[b] = part_ref[b] + moved[b // 2, row:row + 4, :]


def finish_kernel(part_ref, spec_ref, vol_ref, out_ref):
    scale = 1.5 * vol_ref[...]
    for b in range(NF):
        spectral = spec_ref[0, b]
        for j in range(1, PAIRS):
            spectral = spectral + spec_ref[j, b]
        out_ref[b] = part_ref[b] + scale * spectral


def kernel_call(kernel, name, out_shape, in_specs, scratch=(), out_specs=None, limit=2**20, flops=0, moved=0):
    if out_specs is None:
        out_specs = jax.tree.map(lambda _: VMEM, out_shape)
    return pl.pallas_call(
        kernel,
        out_shape=out_shape,
        in_specs=in_specs,
        out_specs=out_specs,
        scratch_shapes=scratch,
        cost_estimate=pl.CostEstimate(flops=flops, bytes_accessed=moved, transcendentals=0),
        compiler_params=pltpu.CompilerParams(vmem_limit_bytes=limit),
        name=name,
    )


def body(adjoint, jac_x, jac_local, objective_gradient, volume, face_lower, face_upper):
    _, _, layers, cells = adjoint.shape
    count = lax.axis_size("space")
    block = NF * layers * cells
    field = jax.ShapeDtypeStruct((NF, layers, cells), jnp.float32)
    face = jax.ShapeDtypeStruct((NF, 2, cells), jnp.float32)
    other = lax.ppermute(adjoint[0], "tm", [(i, i ^ 1) for i in range(NT)])
    own, inner, near, far = kernel_call(
        across_kernel, "across", (field, field, face, face), [HBM, HBM],
        [
            pltpu.VMEM((4, NF, NF, layers, cells), jnp.float32),
            pltpu.VMEM((NF, 8, cells), jnp.float32),
            pltpu.SemaphoreType.DMA((5,)),
        ],
        limit=3 * 2**20, flops=40 * block, moved=84 * block,
    )(pltpu.with_memory_space_constraint(adjoint[0], pltpu.HBM), pltpu.with_memory_space_constraint(jac_x[0], pltpu.HBM))
    far = lax.ppermute(far, "space", [pair for i in range(1, count - 1, 2) for pair in ((i, i + 1), (i + 1, i))])
    combined = kernel_call(
        combine_kernel, "combine", jax.ShapeDtypeStruct((PAIRS, NF, layers, cells), jnp.float32), [VMEM] * 2,
        moved=2000 * block,
    )(own, other)
    groups = [list(range(parity, NT, 2)) for parity in range(2)]
    spectral = lax.all_to_all(combined, "tm", 0, 0, tiled=True, axis_index_groups=groups)
    near, far = kernel_call(after_kernel, "after", (face, face), [VMEM] * 2, flops=10**11, moved=10**8)(near, far)
    near = lax.ppermute(near, "space", [(i, i ^ 1) for i in range(count)])
    part = kernel_call(
        along_kernel, "along", field, [VMEM] * 4, [pltpu.VMEM((2, NF, 8, cells), jnp.float32)],
    )(own, inner, jac_local[0], objective_gradient[0])
    part = kernel_call(
        faces_kernel, "faces", field, [VMEM] * 5,
        [
            pltpu.VMEM(((NF + 1) // 2, 8, cells), jnp.float32),
            pltpu.VMEM(((NF + 1) // 2, 8, cells), jnp.float32),
        ],
        flops=20 * block, moved=20 * block,
    )(part, near, far, face_lower, face_upper)
    out = kernel_call(
        finish_kernel, "finish", field, [VMEM] * 3, flops=5 * block, moved=24 * block,
    )(part, spectral, volume)
    return out[None]


def solution(mesh):
    in_specs = (
        P("tm", None, "space", None),
        P("tm", None, None, None, "space", None),
        P("tm", None, None, None, "space", None),
        P("tm", None, "space", None),
        P("space", None),
        P("space", None),
        P("space", None),
    )
    out_specs = P("tm", None, "space", None)
    return jax.shard_map(body, mesh=mesh, in_specs=in_specs, out_specs=out_specs, check_vma=False)
```

```python
import jax
import jax.numpy as jnp
import numpy as np
from jax import lax
from jax.experimental import pallas as pl
from jax.experimental.pallas import tpu as pltpu
from jax.sharding import PartitionSpec as P

NT = 8
NF = 5
PAIRS = NT // 2
VMEM = pl.BlockSpec(memory_space=pltpu.VMEM)


def spectral_table(count):
    index = np.arange(count)
    offset = index[:, None] - index[None, :]
    parity = np.where(offset % 2 == 0, 1.0, -1.0)
    mask = np.logical_and(offset != 0, np.abs(offset) * 2 != count)
    safe = np.where(mask, offset, 1)
    first = np.where(mask, 0.5 * parity / np.tan(np.pi * safe / count), 0.0)
    apart = offset != 0
    wide = np.where(apart, offset, 1)
    sine = np.sin(np.pi * wide / count)
    second = np.where(apart, -0.5 * parity / (sine * sine), -(count * count + 2) / 12.0)
    return (first + 0.25 * second).astype(np.float32)


def products(fields, blocks, k, b, here):
    total = blocks[k, 0, b, :, here] * fields[0]
    for a in range(1, NF):
        total = total + blocks[k, a, b, :, here] * fields[a]
    return total


def zeros_kernel(out_ref):
    out_ref[...] = jnp.zeros_like(out_ref)


def across_kernel(zeros_ref, own_ref, jac, inner_ref, near_ref, far_ref, ext):
    cells = own_ref.shape[2]
    for at in range(0, cells, 128):
        here = slice(at, at + 128)
        fields = [own_ref[a, :, here] for a in range(NF)]
        for b in range(NF):
            ext[b, :, here] = zeros_ref[...]
            for k, offset in enumerate((1, -1, 2, -2)):
                ext[b, 2 + offset:6 + offset, here] += products(fields, jac, k, b, here)
    even = lax.axis_index("space") % 2 == 0
    for b in range(NF):
        below = ext[b, 0:2, :]
        above = ext[b, 6:8, :]
        inner_ref[b] = ext[b, 2:6, :]
        near_ref[b] = jnp.where(even, above, below)
        far_ref[b] = jnp.where(even, below, above)


def along_kernel(own_ref, inner_ref, jac_ref, obj_ref, part_ref, side):
    cells = own_ref.shape[2]
    side[...] = jnp.zeros_like(side)
    for at in range(0, cells, 128):
        here = slice(at, at + 128)
        fields = [own_ref[a, :, here] for a in range(NF)]
        for b in range(NF):
            part_ref[b, :, here] = obj_ref[b, :, here] + inner_ref[b, :, here] + products(fields, jac_ref, 0, b, here)
            for k in (1, 2):
                side[k - 1, b, 0:4, here] = products(fields, jac_ref, k, b, here)
    lane = lax.broadcasted_iota(jnp.int32, (8, cells), 1)
    for b in range(NF):
        plus = jnp.where(lane == 0, 0.0, pltpu.roll(side[0, b], 1, 1))
        minus = jnp.where(lane == cells - 1, 0.0, pltpu.roll(side[1, b], cells - 1, 1))
        side[0, b] = plus + minus
        part_ref[b] = part_ref[b] + side[0, b, 0:4, :]


def combine_kernel(own_ref, other_ref, out_ref):
    at = lax.axis_index("tm")
    odd = at % 2 == 1
    table = spectral_table(NT)
    for j in range(PAIRS):
        ours = float(table[0, 2 * j])
        theirs = jnp.where(odd, float(table[0, (2 * j + 1) % NT]), float(table[1, 2 * j]))
        out_ref[(at // 2 + j) % PAIRS] = ours * own_ref[...] + theirs * other_ref[...]


def after_kernel(near_ref, far_ref, near_out_ref, far_out_ref):
    near_out_ref[...] = near_ref[...]
    far_out_ref[...] = far_ref[...]


def faces_kernel(part_ref, spec_ref, vol_ref, near_ref, far_ref, low_ref, up_ref, out_ref, halo, moved):
    odd = lax.axis_index("space") % 2 == 1
    cells = low_ref.shape[1]
    halo[...] = jnp.zeros_like(halo)
    sibling = 1 - lax.axis_index("space") % 2
    for b in range(NF):
        row = 4 * (b % 2)
        near = near_ref[sibling, b]
        halo[b // 2, row:row + 2, :] = jnp.where(odd, near, far_ref[b])
        halo[b // 2, row + 2:row + 4, :] = jnp.where(odd, far_ref[b], near)
    groups = halo.shape[0]
    chunks = cells // 128
    from_low = lax.broadcasted_iota(jnp.int32, (8, 128), 0) % 4 < 2
    for j in range(chunks):
        here = slice(128 * j, 128 * (j + 1))
        low = jnp.broadcast_to(low_ref[0:1, here], (8, 128))
        up = jnp.broadcast_to(up_ref[0:1, here], (8, 128))
        index = jnp.where(from_low, low, up)
        lane = index % 128
        chunk = index // 128
        for g in range(groups):
            total = None
            for c in range(chunks):
                piece = jnp.take_along_axis(halo[g, :, 128 * c:128 * (c + 1)], lane, axis=1, mode="promise_in_bounds")
                total = piece if c == 0 else jnp.where(chunk == c, piece, total)
            moved[g, :, here] = total
    scale = 1.5 * vol_ref[...]
    for b in range(NF):
        row = 4 * (b % 2)
        spectral = spec_ref[0, b]
        for j in range(1, PAIRS):
            spectral = spectral + spec_ref[j, b]
        out_ref[b] = part_ref[b] + moved[b // 2, row:row + 4, :] + scale * spectral


def finish_kernel(part_ref, spec_ref, vol_ref, out_ref):
    scale = 1.5 * vol_ref[...]
    for b in range(NF):
        spectral = spec_ref[0, b]
        for j in range(1, PAIRS):
            spectral = spectral + spec_ref[j, b]
        out_ref[b] = part_ref[b] + scale * spectral


def kernel_call(kernel, name, out_shape, in_specs, scratch=(), out_specs=None, limit=2**20, flops=0, moved=0):
    if out_specs is None:
        out_specs = jax.tree.map(lambda _: VMEM, out_shape)
    return pl.pallas_call(
        kernel,
        out_shape=out_shape,
        in_specs=in_specs,
        out_specs=out_specs,
        scratch_shapes=scratch,
        cost_estimate=pl.CostEstimate(flops=flops, bytes_accessed=moved, transcendentals=0),
        compiler_params=pltpu.CompilerParams(vmem_limit_bytes=limit),
        name=name,
    )


def body(adjoint, jac_x, jac_local, objective_gradient, volume, face_lower, face_upper):
    _, _, layers, cells = adjoint.shape
    count = lax.axis_size("space")
    block = NF * layers * cells
    field = jax.ShapeDtypeStruct((NF, layers, cells), jnp.float32)
    face = jax.ShapeDtypeStruct((NF, 2, cells), jnp.float32)
    other = lax.ppermute(adjoint[0], "tm", [(i, i ^ 1) for i in range(NT)])
    zeros = kernel_call(zeros_kernel, "zeros", jax.ShapeDtypeStruct((8, 128), jnp.float32), [], flops=10**11)()
    own = adjoint[0]
    inner, near, far = kernel_call(
        across_kernel, "across", (field, face, face), [VMEM] * 3, [pltpu.VMEM((NF, 8, cells), jnp.float32)],
        flops=40 * block, moved=84 * block,
    )(zeros, own, jac_x[0])
    far = lax.ppermute(far, "space", [pair for i in range(1, count - 1, 2) for pair in ((i, i + 1), (i + 1, i))])
    groups = [list(range(parity, NT, 2)) for parity in range(2)]
    pairs = [[i, i + 1] for i in range(0, count, 2)]
    late = lax.axis_index("space") < 2

    def swap(near):
        return lax.all_gather(near, "space", axis=0, axis_index_groups=pairs)

    def exchange(own, other):
        combined = kernel_call(
            combine_kernel, "combine", jax.ShapeDtypeStruct((PAIRS, NF, layers, cells), jnp.float32), [VMEM] * 2,
            flops=12 * block, moved=24 * block,
        )(own, other)
        return lax.all_to_all(combined, "tm", 0, 0, tiled=True, axis_index_groups=groups)

    def no_swap(near):
        return jnp.zeros((2, *near.shape), near.dtype)

    def in_turn(own, other, near, swapped):
        return exchange(own, other), swapped

    def together(own, other, near, swapped):
        return exchange(own, other), swap(near)

    part = kernel_call(
        along_kernel, "along", field, [VMEM] * 4, [pltpu.VMEM((2, NF, 8, cells), jnp.float32)],
    )(own, inner, jac_local[0], objective_gradient[0])
    swapped = lax.cond(late, swap, no_swap, near)
    spectral, near = lax.cond(late, in_turn, together, own, other, near, swapped)
    out = kernel_call(
        faces_kernel, "faces", field, [VMEM] * 7,
        [
            pltpu.VMEM(((NF + 1) // 2, 8, cells), jnp.float32),
            pltpu.VMEM(((NF + 1) // 2, 8, cells), jnp.float32),
        ],
        flops=20 * block, moved=20 * block,
    )(part, spectral, volume, near, far, face_lower, face_upper)
    return out[None]


def solution(mesh):
    in_specs = (
        P("tm", None, "space", None),
        P("tm", None, None, None, "space", None),
        P("tm", None, None, None, "space", None),
        P("tm", None, "space", None),
        P("space", None),
        P("space", None),
        P("space", None),
    )
    out_specs = P("tm", None, "space", None)
    return jax.shard_map(body, mesh=mesh, in_specs=in_specs, out_specs=out_specs, check_vma=False)
```

```python
import jax
import jax.numpy as jnp
import numpy as np
from jax import lax
from jax.experimental import pallas as pl
from jax.experimental.pallas import tpu as pltpu
from jax.sharding import PartitionSpec as P

NT = 8
NF = 5
PAIRS = NT // 2
VMEM = pl.BlockSpec(memory_space=pltpu.VMEM)


def spectral_table(count):
    index = np.arange(count)
    offset = index[:, None] - index[None, :]
    parity = np.where(offset % 2 == 0, 1.0, -1.0)
    mask = np.logical_and(offset != 0, np.abs(offset) * 2 != count)
    safe = np.where(mask, offset, 1)
    first = np.where(mask, 0.5 * parity / np.tan(np.pi * safe / count), 0.0)
    apart = offset != 0
    wide = np.where(apart, offset, 1)
    sine = np.sin(np.pi * wide / count)
    second = np.where(apart, -0.5 * parity / (sine * sine), -(count * count + 2) / 12.0)
    return (first + 0.25 * second).astype(np.float32)


def products(fields, blocks, k, b, here):
    total = blocks[k, 0, b, :, here] * fields[0]
    for a in range(1, NF):
        total = total + blocks[k, a, b, :, here] * fields[a]
    return total


def zeros_kernel(out_ref):
    out_ref[...] = jnp.zeros_like(out_ref)


def across_kernel(zeros_ref, own_ref, jac, inner_ref, near_ref, far_ref, ext):
    cells = own_ref.shape[2]
    for at in range(0, cells, 128):
        here = slice(at, at + 128)
        fields = [own_ref[a, :, here] for a in range(NF)]
        for b in range(NF):
            ext[b, :, here] = zeros_ref[...]
            for k, offset in enumerate((1, -1, 2, -2)):
                ext[b, 2 + offset:6 + offset, here] += products(fields, jac, k, b, here)
    even = lax.axis_index("space") % 2 == 0
    for b in range(NF):
        below = ext[b, 0:2, :]
        above = ext[b, 6:8, :]
        inner_ref[b] = ext[b, 2:6, :]
        near_ref[b] = jnp.where(even, above, below)
        far_ref[b] = jnp.where(even, below, above)


def along_kernel(own_ref, inner_ref, jac_ref, obj_ref, part_ref, side):
    cells = own_ref.shape[2]
    side[...] = jnp.zeros_like(side)
    for at in range(0, cells, 128):
        here = slice(at, at + 128)
        fields = [own_ref[a, :, here] for a in range(NF)]
        for b in range(NF):
            part_ref[b, :, here] = obj_ref[b, :, here] + inner_ref[b, :, here] + products(fields, jac_ref, 0, b, here)
            for k in (1, 2):
                side[k - 1, b, 0:4, here] = products(fields, jac_ref, k, b, here)
    lane = lax.broadcasted_iota(jnp.int32, (8, cells), 1)
    for b in range(NF):
        plus = jnp.where(lane == 0, 0.0, pltpu.roll(side[0, b], 1, 1))
        minus = jnp.where(lane == cells - 1, 0.0, pltpu.roll(side[1, b], cells - 1, 1))
        side[0, b] = plus + minus
        part_ref[b] = part_ref[b] + side[0, b, 0:4, :]


def combine_kernel(own_ref, other_ref, out_ref):
    at = lax.axis_index("tm")
    odd = at % 2 == 1
    table = spectral_table(NT)
    for j in range(PAIRS):
        ours = float(table[0, 2 * j])
        theirs = jnp.where(odd, float(table[0, (2 * j + 1) % NT]), float(table[1, 2 * j]))
        out_ref[(at // 2 + j) % PAIRS] = ours * own_ref[...] + theirs * other_ref[...]


def after_kernel(near_ref, far_ref, near_out_ref, far_out_ref):
    near_out_ref[...] = near_ref[...]
    far_out_ref[...] = far_ref[...]


def faces_kernel(part_ref, spec_ref, vol_ref, near_ref, far_ref, low_ref, up_ref, out_ref, halo, moved):
    odd = lax.axis_index("space") % 2 == 1
    cells = low_ref.shape[1]
    halo[...] = jnp.zeros_like(halo)
    sibling = 1 - lax.axis_index("space") % 2
    for b in range(NF):
        row = 4 * (b % 2)
        near = near_ref[sibling, b]
        halo[b // 2, row:row + 2, :] = jnp.where(odd, near, far_ref[b])
        halo[b // 2, row + 2:row + 4, :] = jnp.where(odd, far_ref[b], near)
    groups = halo.shape[0]
    chunks = cells // 128
    from_low = lax.broadcasted_iota(jnp.int32, (8, 128), 0) % 4 < 2
    for j in range(chunks):
        here = slice(128 * j, 128 * (j + 1))
        low = jnp.broadcast_to(low_ref[0:1, here], (8, 128))
        up = jnp.broadcast_to(up_ref[0:1, here], (8, 128))
        index = jnp.where(from_low, low, up)
        lane = index % 128
        chunk = index // 128
        for g in range(groups):
            total = None
            for c in range(chunks):
                piece = jnp.take_along_axis(halo[g, :, 128 * c:128 * (c + 1)], lane, axis=1, mode="promise_in_bounds")
                total = piece if c == 0 else jnp.where(chunk == c, piece, total)
            moved[g, :, here] = total
    scale = 1.5 * vol_ref[...]
    for b in range(NF):
        row = 4 * (b % 2)
        spectral = spec_ref[0, b]
        for j in range(1, PAIRS):
            spectral = spectral + spec_ref[j, b]
        out_ref[b] = part_ref[b] + moved[b // 2, row:row + 4, :] + scale * spectral


def finish_kernel(part_ref, spec_ref, vol_ref, out_ref):
    scale = 1.5 * vol_ref[...]
    for b in range(NF):
        spectral = spec_ref[0, b]
        for j in range(1, PAIRS):
            spectral = spectral + spec_ref[j, b]
        out_ref[b] = part_ref[b] + scale * spectral


def kernel_call(kernel, name, out_shape, in_specs, scratch=(), out_specs=None, limit=2**20, flops=0, moved=0):
    if out_specs is None:
        out_specs = jax.tree.map(lambda _: VMEM, out_shape)
    return pl.pallas_call(
        kernel,
        out_shape=out_shape,
        in_specs=in_specs,
        out_specs=out_specs,
        scratch_shapes=scratch,
        cost_estimate=pl.CostEstimate(flops=flops, bytes_accessed=moved, transcendentals=0),
        compiler_params=pltpu.CompilerParams(vmem_limit_bytes=limit),
        name=name,
    )


def body(adjoint, jac_x, jac_local, objective_gradient, volume, face_lower, face_upper):
    _, _, layers, cells = adjoint.shape
    count = lax.axis_size("space")
    block = NF * layers * cells
    field = jax.ShapeDtypeStruct((NF, layers, cells), jnp.float32)
    face = jax.ShapeDtypeStruct((NF, 2, cells), jnp.float32)
    other = lax.ppermute(adjoint[0], "tm", [(i, i ^ 1) for i in range(NT)])
    zeros = kernel_call(zeros_kernel, "zeros", jax.ShapeDtypeStruct((8, 128), jnp.float32), [], flops=10**11)()
    own = adjoint[0]
    inner, near, far = kernel_call(
        across_kernel, "across", (field, face, face), [VMEM] * 3, [pltpu.VMEM((NF, 8, cells), jnp.float32)],
        flops=40 * block, moved=84 * block,
    )(zeros, own, jac_x[0])
    far = lax.ppermute(far, "space", [pair for i in range(1, count - 1, 2) for pair in ((i, i + 1), (i + 1, i))])
    groups = [list(range(parity, NT, 2)) for parity in range(2)]
    pairs = [[i, i + 1] for i in range(0, count, 2)]
    space = lax.axis_index("space")
    edge = jnp.logical_and(space >= 2, jnp.logical_or(space % 8 < 2, space % 8 >= 6))
    late = jnp.logical_not(edge)

    def swap(near):
        return lax.all_gather(near, "space", axis=0, axis_index_groups=pairs)

    def along(own, inner, jac, gradient):
        return kernel_call(
            along_kernel, "along", field, [VMEM] * 4, [pltpu.VMEM((2, NF, 8, cells), jnp.float32)], flops=10**9,
        )(own, inner, jac, gradient)

    def exchange(own, other):
        combined = kernel_call(
            combine_kernel, "combine", jax.ShapeDtypeStruct((PAIRS, NF, layers, cells), jnp.float32), [VMEM] * 2,
            flops=12 * block, moved=24 * block,
        )(own, other)
        return lax.all_to_all(combined, "tm", 0, 0, tiled=True, axis_index_groups=groups)

    def before(near, *local):
        return swap(near), along(*local)

    def not_yet(near, *local):
        return jnp.zeros((2, *near.shape), near.dtype), jnp.zeros_like(own)

    def in_turn(own, other, near, swapped, part, *local):
        return exchange(own, other), swapped, part

    def together(own, other, near, swapped, part, *local):
        return exchange(own, other), swap(near), along(*local)

    local = (own, inner, jac_local[0], objective_gradient[0])
    swapped, part = lax.cond(late, before, not_yet, near, *local)
    spectral, near, part = lax.cond(late, in_turn, together, own, other, near, swapped, part, *local)
    out = kernel_call(
        faces_kernel, "faces", field, [VMEM] * 7,
        [
            pltpu.VMEM(((NF + 1) // 2, 8, cells), jnp.float32),
            pltpu.VMEM(((NF + 1) // 2, 8, cells), jnp.float32),
        ],
        flops=20 * block, moved=20 * block,
    )(part, spectral, volume, near, far, face_lower, face_upper)
    return out[None]


def solution(mesh):
    in_specs = (
        P("tm", None, "space", None),
        P("tm", None, None, None, "space", None),
        P("tm", None, None, None, "space", None),
        P("tm", None, "space", None),
        P("space", None),
        P("space", None),
        P("space", None),
    )
    out_specs = P("tm", None, "space", None)
    return jax.shard_map(body, mesh=mesh, in_specs=in_specs, out_specs=out_specs, check_vma=False)
```

```python
import jax
import jax.numpy as jnp
import numpy as np
from jax import lax
from jax.experimental import pallas as pl
from jax.experimental.pallas import tpu as pltpu
from jax.sharding import PartitionSpec as P

NT = 8
NF = 5
PAIRS = NT // 2
VMEM = pl.BlockSpec(memory_space=pltpu.VMEM)


def spectral_table(count):
    index = np.arange(count)
    offset = index[:, None] - index[None, :]
    parity = np.where(offset % 2 == 0, 1.0, -1.0)
    mask = np.logical_and(offset != 0, np.abs(offset) * 2 != count)
    safe = np.where(mask, offset, 1)
    first = np.where(mask, 0.5 * parity / np.tan(np.pi * safe / count), 0.0)
    apart = offset != 0
    wide = np.where(apart, offset, 1)
    sine = np.sin(np.pi * wide / count)
    second = np.where(apart, -0.5 * parity / (sine * sine), -(count * count + 2) / 12.0)
    return (first + 0.25 * second).astype(np.float32)


def products(fields, blocks, first, b, here):
    total = blocks[first, b, here] * fields[0]
    for a in range(1, NF):
        total = total + blocks[first + a, b, here] * fields[a]
    return total


def zeros_kernel(out_ref):
    out_ref[...] = jnp.zeros_like(out_ref)


def across_kernel(zeros_ref, own_ref, jac_ref, inner_ref, near_ref, far_ref):
    layer = lax.broadcasted_iota(jnp.int32, (8, 128), 0) % 4
    even = lax.axis_index("space") % 2 == 0

    def swapped(rows):
        return jnp.where(layer < 2, pltpu.roll(rows, 6, 0), pltpu.roll(rows, 2, 0))

    for at in range(0, own_ref.shape[1], 8):
        here = slice(at, at + 8)
        fields = [own_ref[a, here, :] for a in range(NF)]
        for b in range(NF):
            up, down, up_2, down_2 = (products(fields, jac_ref, NF * k, b, here) for k in range(4))
            inner = zeros_ref[...] + swapped(jnp.where(layer < 2, up_2, down_2))
            inner = inner + jnp.where(layer >= 1, pltpu.roll(up, 1, 0), 0.0)
            inner = inner + jnp.where(layer <= 2, pltpu.roll(down, 7, 0), 0.0)
            outer = swapped(jnp.where(layer < 2, down_2, up_2))
            outer = outer + jnp.where(layer == 0, pltpu.roll(up, 5, 0), 0.0)
            outer = outer + jnp.where(layer == 3, pltpu.roll(down, 3, 0), 0.0)
            outer = jnp.where(even, outer, swapped(outer))
            inner_ref[b, here, :] = inner
            for half in range(2):
                cells = slice(32 * at + 128 * half, 32 * at + 128 * (half + 1))
                near_ref[b, :, cells] = outer[4 * half:4 * half + 2]
                far_ref[b, :, cells] = outer[4 * half + 2:4 * half + 4]


def read_through(face, index, packed, spread):
    cells = index.shape[1]
    chunks = cells // 128
    row = lax.broadcasted_iota(jnp.int32, (8, 128), 0)
    for b in range(NF - 1):
        packed[0, 2 * b:2 * b + 2, :] = face(b)
    for copy in range(4):
        packed[1, 2 * copy:2 * copy + 2, :] = face(NF - 1)

    def look_up(group, index):
        lane, chunk = index % 128, index // 128
        total = None
        for c in range(chunks):
            piece = jnp.take_along_axis(packed[group, :, 128 * c:128 * (c + 1)], lane, axis=1, mode="promise_in_bounds")
            total = piece if c == 0 else jnp.where(chunk == c, piece, total)
        return total

    wide = [jnp.broadcast_to(index[0:1, 128 * j:128 * (j + 1)], (8, 128)) for j in range(chunks)]
    for j in range(chunks):
        spread[0, :, 128 * j:128 * (j + 1)] = look_up(0, wide[j])
    for start in range(0, chunks, 4):
        mixed = wide[start]
        for copy in range(1, 4):
            mixed = jnp.where(row // 2 == copy, wide[start + copy], mixed)
        total = look_up(1, mixed)
        for copy in range(4):
            spread[1, 0:2, 128 * (start + copy):128 * (start + copy + 1)] = total[2 * copy:2 * copy + 2]
    return [spread[b // 4, 2 * (b % 4):2 * (b % 4) + 2, :] for b in range(NF)]


def add_rows(is_lower, pieces, into):
    @pl.when(is_lower)
    def _():
        for b in range(NF):
            into[b, 0:2, :] += pieces[b]

    @pl.when(jnp.logical_not(is_lower))
    def _():
        for b in range(NF):
            into[b, 2:4, :] += pieces[b]


def along_kernel(own_ref, inner_ref, jac_ref, obj_ref, near_ref, low_ref, up_ref, part_ref, packed, spread):
    groups = range(0, own_ref.shape[1], 8)
    row = lax.broadcasted_iota(jnp.int32, (8, 128), 0)
    lane = lax.broadcasted_iota(jnp.int32, (8, 128), 1)
    nothing = jnp.zeros((8, 128), jnp.float32)
    for b in range(NF):
        center, plus, minus = [], [], []
        for at in groups:
            here = slice(at, at + 8)
            fields = [own_ref[a, here, :] for a in range(NF)]
            center.append(obj_ref[b, here, :] + inner_ref[b, here, :] + products(fields, jac_ref, 0, b, here))
            plus.append(pltpu.roll(products(fields, jac_ref, NF, b, here), 1, 1))
            minus.append(pltpu.roll(products(fields, jac_ref, 2 * NF, b, here), 127, 1))
        across_plus = [nothing] + [pltpu.roll(rows, 4, 0) for rows in plus]
        across_minus = [pltpu.roll(rows, 4, 0) for rows in minus] + [nothing]
        for i, at in enumerate(groups):
            entering = jnp.where(row < 4, across_plus[i], across_plus[i + 1])
            total = center[i] + jnp.where(lane == 0, entering, plus[i])
            entering = jnp.where(row < 4, across_minus[i], across_minus[i + 1])
            total = total + jnp.where(lane == 127, entering, minus[i])
            for half in range(2):
                part_ref[b, :, 32 * at + 128 * half:32 * at + 128 * (half + 1)] = total[4 * half:4 * half + 4]
    odd = lax.axis_index("space") % 2 == 1
    sibling = 1 - lax.axis_index("space") % 2
    index = jnp.where(odd, low_ref[...], up_ref[...])
    add_rows(odd, read_through(lambda b: near_ref[sibling, b], index, packed, spread), part_ref)


def combine_kernel(own_ref, other_ref, out_ref):
    at = lax.axis_index("tm")
    odd = at % 2 == 1
    table = spectral_table(NT)
    for j in range(PAIRS):
        ours = float(table[0, 2 * j])
        theirs = jnp.where(odd, float(table[0, (2 * j + 1) % NT]), float(table[1, 2 * j]))
        out_ref[(at // 2 + j) % PAIRS] = ours * own_ref[...] + theirs * other_ref[...]


def finish_kernel(part_ref, spec_ref, vol_ref, far_ref, low_ref, up_ref, out_ref, packed, spread):
    scale = 1.5 * vol_ref[...]
    for b in range(NF):
        spectral = spec_ref[0, b]
        for j in range(1, PAIRS):
            spectral = spectral + spec_ref[j, b]
        out_ref[b] = part_ref[b] + scale * spectral
    space = lax.axis_index("space")

    @pl.when(jnp.logical_and(space > 0, space < lax.axis_size("space") - 1))
    def _():
        even = space % 2 == 0
        index = jnp.where(even, low_ref[...], up_ref[...])
        add_rows(even, read_through(lambda b: far_ref[b], index, packed, spread), out_ref)


def by_rows(array):
    *lead, layers, cells = array.shape
    split = array.reshape(-1, layers, cells // 128, 128).transpose(0, 2, 1, 3)
    return split.reshape(-1, layers * cells // 128, 128)


def kernel_call(kernel, name, out_shape, in_specs, scratch=(), out_specs=None, limit=2**20, flops=0, moved=0):
    if out_specs is None:
        out_specs = jax.tree.map(lambda _: VMEM, out_shape)
    return pl.pallas_call(
        kernel,
        out_shape=out_shape,
        in_specs=in_specs,
        out_specs=out_specs,
        scratch_shapes=scratch,
        cost_estimate=pl.CostEstimate(flops=flops, bytes_accessed=moved, transcendentals=0),
        compiler_params=pltpu.CompilerParams(vmem_limit_bytes=limit),
        name=name,
    )


def body(adjoint, jac_x, jac_local, objective_gradient, volume, face_lower, face_upper):
    _, _, layers, cells = adjoint.shape
    count = lax.axis_size("space")
    block = NF * layers * cells
    field = jax.ShapeDtypeStruct((NF, layers, cells), jnp.float32)
    face = jax.ShapeDtypeStruct((NF, 2, cells), jnp.float32)
    other = lax.ppermute(adjoint[0], "tm", [(i, i ^ 1) for i in range(NT)])
    rows = jax.ShapeDtypeStruct((NF, layers * cells // 128, 128), jnp.float32)
    zeros = kernel_call(zeros_kernel, "zeros", jax.ShapeDtypeStruct((8, 128), jnp.float32), [], flops=10**11)()
    own = adjoint[0]
    inner, near, far = kernel_call(
        across_kernel, "across", (rows, face, face), [VMEM] * 3, flops=40 * block, moved=84 * block,
    )(zeros, by_rows(own), by_rows(jac_x[0]).reshape(4 * NF, NF, -1, 128))
    far = lax.ppermute(far, "space", [pair for i in range(1, count - 1, 2) for pair in ((i, i + 1), (i + 1, i))])
    groups = [list(range(parity, NT, 2)) for parity in range(2)]
    pairs = [[i, i + 1] for i in range(0, count, 2)]
    gathering = [pltpu.VMEM((2, 8, cells), jnp.float32)] * 2

    def along(own, inner, near, jac, gradient, low, up):
        near = lax.all_gather(near, "space", axis=0, axis_index_groups=pairs)
        return kernel_call(
            along_kernel, "along", field, [VMEM] * 7, gathering, flops=10**9,
        )(by_rows(own), inner, by_rows(jac).reshape(3 * NF, NF, -1, 128), by_rows(gradient), near, low, up)

    def exchange(own, other):
        combined = kernel_call(
            combine_kernel, "combine", jax.ShapeDtypeStruct((PAIRS, NF, layers, cells), jnp.float32), [VMEM] * 2,
            flops=12 * block, moved=24 * block,
        )(own, other)
        return lax.all_to_all(combined, "tm", 0, 0, tiled=True, axis_index_groups=groups)

    def not_yet(*local):
        return jnp.zeros_like(own)

    def in_turn(own, other, part, *local):
        return exchange(own, other), part

    def together(own, other, part, *local):
        return exchange(own, other), along(*local)

    space = lax.axis_index("space")
    edge = jnp.logical_and(space >= 2, jnp.logical_or(space % 8 < 2, space % 8 >= 6))
    middle = jnp.logical_and(space // 8 == count // 16 - 1, space % 8 >= 6)
    edge = jnp.logical_and(edge, jnp.logical_or(lax.axis_index("tm") % 2 == 0, middle))
    local = (own, inner, near, jac_local[0], objective_gradient[0], face_lower, face_upper)
    part = lax.cond(jnp.logical_not(edge), along, not_yet, *local)
    spectral, part = lax.cond(jnp.logical_not(edge), in_turn, together, own, other, part, *local)
    out = kernel_call(
        finish_kernel, "finish", field, [VMEM] * 6, gathering, flops=20 * block, moved=20 * block,
    )(part, spectral, volume, far, face_lower, face_upper)
    return out[None]


def solution(mesh):
    in_specs = (
        P("tm", None, "space", None),
        P("tm", None, None, None, "space", None),
        P("tm", None, None, None, "space", None),
        P("tm", None, "space", None),
        P("space", None),
        P("space", None),
        P("space", None),
    )
    out_specs = P("tm", None, "space", None)
    return jax.shard_map(body, mesh=mesh, in_specs=in_specs, out_specs=out_specs, check_vma=False)
```

```python
import jax
import jax.numpy as jnp
import numpy as np
from jax import lax
from jax.experimental import pallas as pl
from jax.experimental.pallas import tpu as pltpu
from jax.sharding import PartitionSpec as P

NT = 8
NF = 5
PAIRS = NT // 2
ORDER = (0, 3, 1, 2)
VMEM = pl.BlockSpec(memory_space=pltpu.VMEM)


def spectral_table(count):
    index = np.arange(count)
    offset = index[:, None] - index[None, :]
    parity = np.where(offset % 2 == 0, 1.0, -1.0)
    mask = np.logical_and(offset != 0, np.abs(offset) * 2 != count)
    safe = np.where(mask, offset, 1)
    first = np.where(mask, 0.5 * parity / np.tan(np.pi * safe / count), 0.0)
    apart = offset != 0
    wide = np.where(apart, offset, 1)
    sine = np.sin(np.pi * wide / count)
    second = np.where(apart, -0.5 * parity / (sine * sine), -(count * count + 2) / 12.0)
    return (first + 0.25 * second).astype(np.float32)


def products(fields, blocks, first, b, here):
    total = blocks[first, b, here] * fields[0]
    for a in range(1, NF):
        total = total + blocks[first + a, b, here] * fields[a]
    return total


def zeros_kernel(out_ref):
    out_ref[...] = jnp.zeros_like(out_ref)


def across_kernel(zeros_ref, own_ref, jac_ref, inner_ref, near_ref, far_ref):
    layer = lax.broadcasted_iota(jnp.int32, (8, 128), 0) % 4
    even = lax.axis_index("space") % 2 == 0

    def swapped(rows):
        return jnp.where(layer < 2, pltpu.roll(rows, 6, 0), pltpu.roll(rows, 2, 0))

    for at in range(0, own_ref.shape[1], 8):
        here = slice(at, at + 8)
        fields = [own_ref[a, here, :] for a in range(NF)]
        for b in range(NF):
            up, down, up_2, down_2 = (products(fields, jac_ref, NF * k, b, here) for k in range(4))
            inner = zeros_ref[...] + swapped(jnp.where(layer < 2, up_2, down_2))
            inner = inner + jnp.where(layer >= 1, pltpu.roll(up, 1, 0), 0.0)
            inner = inner + jnp.where(layer <= 2, pltpu.roll(down, 7, 0), 0.0)
            outer = swapped(jnp.where(layer < 2, down_2, up_2))
            outer = outer + jnp.where(layer == 0, pltpu.roll(up, 5, 0), 0.0)
            outer = outer + jnp.where(layer == 3, pltpu.roll(down, 3, 0), 0.0)
            outer = jnp.where(even, outer, swapped(outer))
            inner_ref[b, here, :] = inner
            for half in range(2):
                cells = slice(32 * at + 128 * half, 32 * at + 128 * (half + 1))
                near_ref[b, :, cells] = outer[4 * half:4 * half + 2]
                far_ref[b, :, cells] = outer[4 * half + 2:4 * half + 4]


def read_through(face, index, packed, spread):
    cells = index.shape[1]
    chunks = cells // 128
    row = lax.broadcasted_iota(jnp.int32, (8, 128), 0)
    for b in range(NF - 1):
        packed[0, 2 * b:2 * b + 2, :] = face(b)
    for copy in range(4):
        packed[1, 2 * copy:2 * copy + 2, :] = face(NF - 1)

    def look_up(group, index):
        lane, chunk = index % 128, index // 128
        total = None
        for c in range(chunks):
            piece = jnp.take_along_axis(packed[group, :, 128 * c:128 * (c + 1)], lane, axis=1, mode="promise_in_bounds")
            total = piece if c == 0 else jnp.where(chunk == c, piece, total)
        return total

    wide = [jnp.broadcast_to(index[0:1, 128 * j:128 * (j + 1)], (8, 128)) for j in range(chunks)]
    for j in range(chunks):
        spread[0, :, 128 * j:128 * (j + 1)] = look_up(0, wide[j])
    for start in range(0, chunks, 4):
        mixed = wide[start]
        for copy in range(1, 4):
            mixed = jnp.where(row // 2 == copy, wide[start + copy], mixed)
        total = look_up(1, mixed)
        for copy in range(4):
            spread[1, 0:2, 128 * (start + copy):128 * (start + copy + 1)] = total[2 * copy:2 * copy + 2]
    return [spread[b // 4, 2 * (b % 4):2 * (b % 4) + 2, :] for b in range(NF)]


def add_rows(is_lower, pieces, into):
    @pl.when(is_lower)
    def _():
        for b in range(NF):
            into[b, 0:2, :] += pieces[b]

    @pl.when(jnp.logical_not(is_lower))
    def _():
        for b in range(NF):
            into[b, 2:4, :] += pieces[b]


def along_kernel(own_ref, inner_ref, jac_ref, obj_ref, near_ref, low_ref, up_ref, part_ref, packed, spread):
    groups = range(0, own_ref.shape[1], 8)
    row = lax.broadcasted_iota(jnp.int32, (8, 128), 0)
    lane = lax.broadcasted_iota(jnp.int32, (8, 128), 1)
    nothing = jnp.zeros((8, 128), jnp.float32)
    for b in range(NF):
        center, plus, minus = [], [], []
        for at in groups:
            here = slice(at, at + 8)
            fields = [own_ref[a, here, :] for a in range(NF)]
            center.append(obj_ref[b, here, :] + inner_ref[b, here, :] + products(fields, jac_ref, 0, b, here))
            plus.append(pltpu.roll(products(fields, jac_ref, NF, b, here), 1, 1))
            minus.append(pltpu.roll(products(fields, jac_ref, 2 * NF, b, here), 127, 1))
        across_plus = [nothing] + [pltpu.roll(rows, 4, 0) for rows in plus]
        across_minus = [pltpu.roll(rows, 4, 0) for rows in minus] + [nothing]
        for i, at in enumerate(groups):
            entering = jnp.where(row < 4, across_plus[i], across_plus[i + 1])
            total = center[i] + jnp.where(lane == 0, entering, plus[i])
            entering = jnp.where(row < 4, across_minus[i], across_minus[i + 1])
            total = total + jnp.where(lane == 127, entering, minus[i])
            for half in range(2):
                part_ref[b, :, 32 * at + 128 * half:32 * at + 128 * (half + 1)] = total[4 * half:4 * half + 4]
    odd = lax.axis_index("space") % 2 == 1
    sibling = 1 - lax.axis_index("space") % 2
    index = jnp.where(odd, low_ref[...], up_ref[...])
    add_rows(odd, read_through(lambda b: near_ref[sibling, b], index, packed, spread), part_ref)


def combine_kernel(own_ref, other_ref, out_ref):
    at = lax.axis_index("tm")
    odd = at % 2 == 1
    table = spectral_table(NT)
    for j in range(PAIRS):
        ours = float(table[0, 2 * j])
        theirs = jnp.where(odd, float(table[0, (2 * j + 1) % NT]), float(table[1, 2 * j]))
        pair = (at // 2 + j) % PAIRS
        slot = 0
        for place, member in enumerate(ORDER):
            slot = jnp.where(pair == member, place, slot)
        out_ref[slot] = ours * own_ref[...] + theirs * other_ref[...]


def finish_kernel(part_ref, spec_ref, vol_ref, far_ref, low_ref, up_ref, out_ref, packed, spread):
    scale = 1.5 * vol_ref[...]
    for b in range(NF):
        spectral = spec_ref[0, b]
        for j in range(1, PAIRS):
            spectral = spectral + spec_ref[j, b]
        out_ref[b] = part_ref[b] + scale * spectral
    space = lax.axis_index("space")

    @pl.when(jnp.logical_and(space > 0, space < lax.axis_size("space") - 1))
    def _():
        even = space % 2 == 0
        index = jnp.where(even, low_ref[...], up_ref[...])
        add_rows(even, read_through(lambda b: far_ref[b], index, packed, spread), out_ref)


def by_rows(array):
    *lead, layers, cells = array.shape
    split = array.reshape(-1, layers, cells // 128, 128).transpose(0, 2, 1, 3)
    return split.reshape(-1, layers * cells // 128, 128)


def kernel_call(kernel, name, out_shape, in_specs, scratch=(), out_specs=None, limit=2**20, flops=0, moved=0):
    if out_specs is None:
        out_specs = jax.tree.map(lambda _: VMEM, out_shape)
    return pl.pallas_call(
        kernel,
        out_shape=out_shape,
        in_specs=in_specs,
        out_specs=out_specs,
        scratch_shapes=scratch,
        cost_estimate=pl.CostEstimate(flops=flops, bytes_accessed=moved, transcendentals=0),
        compiler_params=pltpu.CompilerParams(vmem_limit_bytes=limit),
        name=name,
    )


def body(adjoint, jac_x, jac_local, objective_gradient, volume, face_lower, face_upper):
    _, _, layers, cells = adjoint.shape
    count = lax.axis_size("space")
    block = NF * layers * cells
    field = jax.ShapeDtypeStruct((NF, layers, cells), jnp.float32)
    face = jax.ShapeDtypeStruct((NF, 2, cells), jnp.float32)
    other = lax.ppermute(adjoint[0], "tm", [(i, i ^ 1) for i in range(NT)])
    rows = jax.ShapeDtypeStruct((NF, layers * cells // 128, 128), jnp.float32)
    zeros = kernel_call(zeros_kernel, "zeros", jax.ShapeDtypeStruct((8, 128), jnp.float32), [], flops=10**11)()
    own = adjoint[0]
    inner, near, far = kernel_call(
        across_kernel, "across", (rows, face, face), [VMEM] * 3, flops=40 * block, moved=84 * block,
    )(zeros, by_rows(own), by_rows(jac_x[0]).reshape(4 * NF, NF, -1, 128))
    far = lax.ppermute(far, "space", [pair for i in range(1, count - 1, 2) for pair in ((i, i + 1), (i + 1, i))])
    groups = [[2 * pair + parity for pair in ORDER] for parity in range(2)]
    pairs = [[i, i + 1] for i in range(0, count, 2)]
    gathering = [pltpu.VMEM((2, 8, cells), jnp.float32)] * 2

    def along(own, inner, near, jac, gradient, low, up):
        near = lax.all_gather(near, "space", axis=0, axis_index_groups=pairs)
        return kernel_call(
            along_kernel, "along", field, [VMEM] * 7, gathering, flops=10**9,
        )(by_rows(own), inner, by_rows(jac).reshape(3 * NF, NF, -1, 128), by_rows(gradient), near, low, up)

    def exchange(own, other):
        combined = kernel_call(
            combine_kernel, "combine", jax.ShapeDtypeStruct((PAIRS, NF, layers, cells), jnp.float32), [VMEM] * 2,
            flops=12 * block, moved=24 * block,
        )(own, other)
        return lax.all_to_all(combined, "tm", 0, 0, tiled=True, axis_index_groups=groups)

    def not_yet(*local):
        return jnp.zeros_like(own)

    def in_turn(own, other, part, *local):
        return exchange(own, other), part

    def together(own, other, part, *local):
        return exchange(own, other), along(*local)

    space = lax.axis_index("space")
    edge = jnp.logical_and(space >= 2, jnp.logical_or(space % 8 < 2, space % 8 >= 6))
    middle = jnp.logical_and(space // 8 == count // 16 - 1, space % 8 >= 6)
    edge = jnp.logical_and(edge, jnp.logical_or(lax.axis_index("tm") % 2 == 0, middle))
    local = (own, inner, near, jac_local[0], objective_gradient[0], face_lower, face_upper)
    part = lax.cond(jnp.logical_not(edge), along, not_yet, *local)
    spectral, part = lax.cond(jnp.logical_not(edge), in_turn, together, own, other, part, *local)
    out = kernel_call(
        finish_kernel, "finish", field, [VMEM] * 6, gathering, flops=20 * block, moved=20 * block,
    )(part, spectral, volume, far, face_lower, face_upper)
    return out[None]


def solution(mesh):
    in_specs = (
        P("tm", None, "space", None),
        P("tm", None, None, None, "space", None),
        P("tm", None, None, None, "space", None),
        P("tm", None, "space", None),
        P("space", None),
        P("space", None),
        P("space", None),
    )
    out_specs = P("tm", None, "space", None)
    return jax.shard_map(body, mesh=mesh, in_specs=in_specs, out_specs=out_specs, check_vma=False)
```

```python
import functools

import jax
import jax.numpy as jnp
import numpy as np
from jax import lax
from jax.experimental import pallas as pl
from jax.experimental.pallas import tpu as pltpu
from jax.sharding import PartitionSpec as P

NT = 8
NF = 5
PAIRS = NT // 2
ORDER = (0, 3, 1, 2)
ORDER_BESIDE = (0, 2, 1, 3)
VMEM = pl.BlockSpec(memory_space=pltpu.VMEM)


def spectral_table(count):
    index = np.arange(count)
    offset = index[:, None] - index[None, :]
    parity = np.where(offset % 2 == 0, 1.0, -1.0)
    mask = np.logical_and(offset != 0, np.abs(offset) * 2 != count)
    safe = np.where(mask, offset, 1)
    first = np.where(mask, 0.5 * parity / np.tan(np.pi * safe / count), 0.0)
    apart = offset != 0
    wide = np.where(apart, offset, 1)
    sine = np.sin(np.pi * wide / count)
    second = np.where(apart, -0.5 * parity / (sine * sine), -(count * count + 2) / 12.0)
    return (first + 0.25 * second).astype(np.float32)


def products(fields, blocks, first, b, here):
    total = blocks[first, b, here] * fields[0]
    for a in range(1, NF):
        total = total + blocks[first + a, b, here] * fields[a]
    return total


def zeros_kernel(out_ref):
    out_ref[...] = jnp.zeros_like(out_ref)


def across_kernel(zeros_ref, own_ref, jac_ref, inner_ref, near_ref, far_ref):
    layer = lax.broadcasted_iota(jnp.int32, (8, 128), 0) % 4
    even = lax.axis_index("space") % 2 == 0

    def swapped(rows):
        return jnp.where(layer < 2, pltpu.roll(rows, 6, 0), pltpu.roll(rows, 2, 0))

    for at in range(0, own_ref.shape[1], 8):
        here = slice(at, at + 8)
        fields = [own_ref[a, here, :] for a in range(NF)]
        for b in range(NF):
            up, down, up_2, down_2 = (products(fields, jac_ref, NF * k, b, here) for k in range(4))
            inner = zeros_ref[...] + swapped(jnp.where(layer < 2, up_2, down_2))
            inner = inner + jnp.where(layer >= 1, pltpu.roll(up, 1, 0), 0.0)
            inner = inner + jnp.where(layer <= 2, pltpu.roll(down, 7, 0), 0.0)
            outer = swapped(jnp.where(layer < 2, down_2, up_2))
            outer = outer + jnp.where(layer == 0, pltpu.roll(up, 5, 0), 0.0)
            outer = outer + jnp.where(layer == 3, pltpu.roll(down, 3, 0), 0.0)
            outer = jnp.where(even, outer, swapped(outer))
            inner_ref[b, here, :] = inner
            for half in range(2):
                cells = slice(32 * at + 128 * half, 32 * at + 128 * (half + 1))
                near_ref[b, :, cells] = outer[4 * half:4 * half + 2]
                far_ref[b, :, cells] = outer[4 * half + 2:4 * half + 4]


def read_through(face, index, packed, spread):
    cells = index.shape[1]
    chunks = cells // 128
    row = lax.broadcasted_iota(jnp.int32, (8, 128), 0)
    for b in range(NF - 1):
        packed[0, 2 * b:2 * b + 2, :] = face(b)
    for copy in range(4):
        packed[1, 2 * copy:2 * copy + 2, :] = face(NF - 1)

    def look_up(group, index):
        lane, chunk = index % 128, index // 128
        total = None
        for c in range(chunks):
            piece = jnp.take_along_axis(packed[group, :, 128 * c:128 * (c + 1)], lane, axis=1, mode="promise_in_bounds")
            total = piece if c == 0 else jnp.where(chunk == c, piece, total)
        return total

    wide = [jnp.broadcast_to(index[0:1, 128 * j:128 * (j + 1)], (8, 128)) for j in range(chunks)]
    for j in range(chunks):
        spread[0, :, 128 * j:128 * (j + 1)] = look_up(0, wide[j])
    for start in range(0, chunks, 4):
        mixed = wide[start]
        for copy in range(1, 4):
            mixed = jnp.where(row // 2 == copy, wide[start + copy], mixed)
        total = look_up(1, mixed)
        for copy in range(4):
            spread[1, 0:2, 128 * (start + copy):128 * (start + copy + 1)] = total[2 * copy:2 * copy + 2]
    return [spread[b // 4, 2 * (b % 4):2 * (b % 4) + 2, :] for b in range(NF)]


def add_rows(is_lower, pieces, into):
    @pl.when(is_lower)
    def _():
        for b in range(NF):
            into[b, 0:2, :] += pieces[b]

    @pl.when(jnp.logical_not(is_lower))
    def _():
        for b in range(NF):
            into[b, 2:4, :] += pieces[b]


def along_kernel(own_ref, inner_ref, jac_ref, obj_ref, near_ref, low_ref, up_ref, part_ref, packed, spread):
    groups = range(0, own_ref.shape[1], 8)
    row = lax.broadcasted_iota(jnp.int32, (8, 128), 0)
    lane = lax.broadcasted_iota(jnp.int32, (8, 128), 1)
    nothing = jnp.zeros((8, 128), jnp.float32)
    for b in range(NF):
        center, plus, minus = [], [], []
        for at in groups:
            here = slice(at, at + 8)
            fields = [own_ref[a, here, :] for a in range(NF)]
            center.append(obj_ref[b, here, :] + inner_ref[b, here, :] + products(fields, jac_ref, 0, b, here))
            plus.append(pltpu.roll(products(fields, jac_ref, NF, b, here), 1, 1))
            minus.append(pltpu.roll(products(fields, jac_ref, 2 * NF, b, here), 127, 1))
        across_plus = [nothing] + [pltpu.roll(rows, 4, 0) for rows in plus]
        across_minus = [pltpu.roll(rows, 4, 0) for rows in minus] + [nothing]
        for i, at in enumerate(groups):
            entering = jnp.where(row < 4, across_plus[i], across_plus[i + 1])
            total = center[i] + jnp.where(lane == 0, entering, plus[i])
            entering = jnp.where(row < 4, across_minus[i], across_minus[i + 1])
            total = total + jnp.where(lane == 127, entering, minus[i])
            for half in range(2):
                part_ref[b, :, 32 * at + 128 * half:32 * at + 128 * (half + 1)] = total[4 * half:4 * half + 4]
    odd = lax.axis_index("space") % 2 == 1
    sibling = 1 - lax.axis_index("space") % 2
    index = jnp.where(odd, low_ref[...], up_ref[...])
    add_rows(odd, read_through(lambda b: near_ref[sibling, b], index, packed, spread), part_ref)


def combine_kernel(order, own_ref, other_ref, out_ref):
    at = lax.axis_index("tm")
    odd = at % 2 == 1
    table = spectral_table(NT)
    for j in range(PAIRS):
        ours = float(table[0, 2 * j])
        theirs = jnp.where(odd, float(table[0, (2 * j + 1) % NT]), float(table[1, 2 * j]))
        pair = (at // 2 + j) % PAIRS
        slot = 0
        for place, member in enumerate(order):
            slot = jnp.where(pair == member, place, slot)
        out_ref[slot] = ours * own_ref[...] + theirs * other_ref[...]


def finish_kernel(part_ref, spec_ref, vol_ref, far_ref, low_ref, up_ref, out_ref, packed, spread):
    scale = 1.5 * vol_ref[...]
    for b in range(NF):
        spectral = spec_ref[0, b]
        for j in range(1, PAIRS):
            spectral = spectral + spec_ref[j, b]
        out_ref[b] = part_ref[b] + scale * spectral
    space = lax.axis_index("space")

    @pl.when(jnp.logical_and(space > 0, space < lax.axis_size("space") - 1))
    def _():
        even = space % 2 == 0
        index = jnp.where(even, low_ref[...], up_ref[...])
        add_rows(even, read_through(lambda b: far_ref[b], index, packed, spread), out_ref)


def by_rows(array):
    *lead, layers, cells = array.shape
    split = array.reshape(-1, layers, cells // 128, 128).transpose(0, 2, 1, 3)
    return split.reshape(-1, layers * cells // 128, 128)


def by_cells(rows, layers):
    split = rows.reshape(rows.shape[0], -1, layers, 128).transpose(0, 2, 1, 3)
    return split.reshape(rows.shape[0], layers, -1)


def kernel_call(kernel, name, out_shape, in_specs, scratch=(), out_specs=None, limit=2**20, flops=0, moved=0):
    if out_specs is None:
        out_specs = jax.tree.map(lambda _: VMEM, out_shape)
    return pl.pallas_call(
        kernel,
        out_shape=out_shape,
        in_specs=in_specs,
        out_specs=out_specs,
        scratch_shapes=scratch,
        cost_estimate=pl.CostEstimate(flops=flops, bytes_accessed=moved, transcendentals=0),
        compiler_params=pltpu.CompilerParams(vmem_limit_bytes=limit),
        name=name,
    )


def body(adjoint, jac_x, jac_local, objective_gradient, volume, face_lower, face_upper):
    _, _, layers, cells = adjoint.shape
    count = lax.axis_size("space")
    block = NF * layers * cells
    field = jax.ShapeDtypeStruct((NF, layers, cells), jnp.float32)
    face = jax.ShapeDtypeStruct((NF, 2, cells), jnp.float32)
    other = lax.ppermute(adjoint[0], "tm", [(i, i ^ 1) for i in range(NT)])
    rows = jax.ShapeDtypeStruct((NF, layers * cells // 128, 128), jnp.float32)
    zeros = kernel_call(zeros_kernel, "zeros", jax.ShapeDtypeStruct((8, 128), jnp.float32), [], flops=10**11)()
    own = adjoint[0]
    inner, near, far = kernel_call(
        across_kernel, "across", (rows, face, face), [VMEM] * 3, flops=40 * block, moved=84 * block,
    )(zeros, by_rows(own), by_rows(jac_x[0]).reshape(4 * NF, NF, -1, 128))
    far = lax.ppermute(far, "space", [pair for i in range(1, count - 1, 2) for pair in ((i, i + 1), (i + 1, i))])
    pairs = [[i, i + 1] for i in range(0, count, 2)]
    gathering = [pltpu.VMEM((2, 8, cells), jnp.float32)] * 2

    def along(own, inner, near, jac, gradient, low, up):
        near = lax.all_gather(near, "space", axis=0, axis_index_groups=pairs)
        return kernel_call(
            along_kernel, "along", field, [VMEM] * 7, gathering, flops=10**9,
        )(by_rows(own), inner, by_rows(jac).reshape(3 * NF, NF, -1, 128), by_rows(gradient), near, low, up)

    def exchange(order, own, other):
        groups = [[2 * pair + parity for pair in order] for parity in range(2)]
        combined = kernel_call(
            functools.partial(combine_kernel, order), "combine", jax.ShapeDtypeStruct((PAIRS, NF, layers, cells), jnp.float32), [VMEM] * 2,
            flops=12 * block, moved=24 * block,
        )(own, other)
        sent = by_rows(combined).reshape(PAIRS, -1, 128)
        got = lax.all_to_all(sent, "tm", 0, 0, tiled=True, axis_index_groups=groups)
        return by_cells(got.reshape(PAIRS * NF, -1, 128), layers).reshape(PAIRS, NF, layers, cells)

    def not_yet(*local):
        return jnp.zeros_like(own)

    def in_turn(own, other, part, *local):
        return exchange(ORDER, own, other), part

    def together(own, other, part, *local):
        return exchange(ORDER_BESIDE, own, other), along(*local)

    space = lax.axis_index("space")
    edge = jnp.logical_and(space >= 2, jnp.logical_or(space % 8 < 2, space % 8 >= 6))
    middle = jnp.logical_and(space // 8 == count // 16 - 1, space % 8 >= 6)
    edge = jnp.logical_and(edge, jnp.logical_or(lax.axis_index("tm") % 2 == 0, middle))
    local = (own, inner, near, jac_local[0], objective_gradient[0], face_lower, face_upper)
    part = lax.cond(jnp.logical_not(edge), along, not_yet, *local)
    spectral, part = lax.cond(jnp.logical_not(edge), in_turn, together, own, other, part, *local)
    out = kernel_call(
        finish_kernel, "finish", field, [VMEM] * 6, gathering, flops=20 * block, moved=20 * block,
    )(part, spectral, volume, far, face_lower, face_upper)
    return out[None]


def solution(mesh):
    in_specs = (
        P("tm", None, "space", None),
        P("tm", None, None, None, "space", None),
        P("tm", None, None, None, "space", None),
        P("tm", None, "space", None),
        P("space", None),
        P("space", None),
        P("space", None),
    )
    out_specs = P("tm", None, "space", None)
    return jax.shard_map(body, mesh=mesh, in_specs=in_specs, out_specs=out_specs, check_vma=False)
```
